32 devices in a mesh: lat: 4 (over y, x), grid: 8 (over z, core).
Axes of the slice: x: 2, y: 2, z: 4, core: 2. Of those that a mesh axis runs over, the one named last changes fastest.
Arguments:
- grid_state: bfloat16 [192, 1280, 4096], P(None, 'lat', 'grid'), may hold values from -6 to 6
- radiation: bfloat16 [192, 192], replicated, may hold values from -0.4375 to 0.4375
- cloud_slots: int32 [4, 8, 8, 512], P('lat', 'grid'), may hold values from 0 to 163840, as said below
- wave_order: int32 [640], replicated, may hold values from 0 to 639, each once
- legendre: bfloat16 [640, 1280, 640], P(('lat', 'grid')), may hold values from -0.15625 to 0.15625
Outputs:
- spectral: bfloat16 [640, 384, 640], P(('lat', 'grid'))
The draws below stay inside these ranges and needn't reach their ends.
Inputs may be any that keep to these rules, and one draw needn't show every extreme that they name: cloud_slots[l, g, h, s] is a column index of device (l, g) among its 163840 columns, and helper h of the band is the one listed for it; the value 163840 marks an empty slot; no column is listed twice by one device. `wave_order`: each wavenumber stands in exactly one slot.
All inputs are finite; a program needn't handle non-finite values.
Results may differ from the reference program's by a relative error of at most 0.0058.
Values may be sent and summed in bfloat16 or wider, within the bound.
No kernel may reach another device: no remote copies, remote signals or barrier semaphores. Data moves between devices by JAX's collectives and lax.ppermute only.
A program may use at most 384 MiB of HBM per device.

```python
import math
import jax
import jax.numpy as jnp
from jax import lax

NLAT = 1280
NLON = 4096
WAVES = 640
FL = 192
SCAP = 512
COLS_DEV = 163840
N_LAT = 4
N_GRID = 8


def draw_cloud_slots(key, part):
    devices = N_LAT * N_GRID
    key_order, key_count, key_level, key_full = jax.random.split(key, 4)
    device_keys = jax.random.split(key_order, devices)

    def first_columns(device_key):
        return jax.random.permutation(device_key, COLS_DEV)[:N_GRID * SCAP]
    chosen = jax.vmap(first_columns)(device_keys).reshape(devices, N_GRID, SCAP)
    level_drawn = jax.random.randint(key_level, (devices, 1), 0, 4)
    raw_counts = jax.random.randint(key_count, (devices, N_GRID), 0, SCAP + 1)
    slot_counts = jnp.minimum(SCAP, raw_counts * (level_drawn + 1) // 2)
    full_helper = jax.random.randint(key_full, (), 0, N_GRID)
    slot_counts = jnp.where(jnp.arange(N_GRID)[None, :] == full_helper, SCAP, slot_counts)
    is_live = jnp.arange(SCAP)[None, None, :] < slot_counts[:, :, None]
    listed = jnp.where(is_live, chosen, COLS_DEV)
    return listed.reshape(N_LAT, N_GRID, N_GRID, SCAP).astype(jnp.int32)


def level_of(rng, dims, pieces, smallest, top_value):
    def one(position, blocks):
        heights = jax.random.uniform(jax.random.fold_in(jax.random.fold_in(rng, 6), position), (blocks,), jnp.float32, smallest / len(pieces), top_value / len(pieces))
        return jnp.repeat(jnp.exp(heights), dims[position] // blocks).reshape((-1,) + (1,) * (len(dims) - position - 1))

    factor_of = one(*pieces[0])
    for cut in pieces[1:]:
        factor_of = factor_of * one(*cut)
    return factor_of


def gaussian(stream_key, extent, deviation, reach, cuts=(), kind=jnp.bfloat16):
    entries = deviation * jax.random.normal(stream_key, extent, jnp.float32)
    if cuts:
        entries = entries * level_of(stream_key, extent, cuts, -0.22, 0.18)
    return jnp.clip(entries, -reach, reach).astype(kind)


def setup_inputs(seed: int = 0) -> dict:
    splits = jax.random.split(jax.random.key(seed), 6)
    return {
        "grid_state": gaussian(splits[0], (FL, NLAT, NLON), 1.0, 6.0, ((1, 4), (2, 8))),
        "radiation": gaussian(splits[1], (FL, FL), FL ** -0.5, 0.4375),
        "cloud_slots": draw_cloud_slots(jax.random.fold_in(splits[5], 71), 0),
        "wave_order": jax.random.permutation(splits[3], WAVES).astype(jnp.int32),
        "legendre": gaussian(splits[4], (WAVES, NLAT, WAVES), NLAT ** -0.5, 0.15625, ((0, 32),)),
    }


def fourier_table(wave_order, nlon):
    longitude = jnp.arange(nlon, dtype=jnp.int32)
    phases = wave_order[:, None] * longitude[None, :] % nlon
    angles = phases.astype(jnp.float32) * (2.0 * math.pi / nlon)
    return jnp.stack([jnp.cos(angles), -jnp.sin(angles)]).astype(jnp.bfloat16)

def reference(grid_state, radiation, cloud_slots, wave_order, legendre):
    levels, nlat, nlon = grid_state.shape
    band_rows = nlat // N_LAT
    lon_width = nlon // N_GRID
    columns = band_rows * lon_width
    lat_index = jnp.arange(N_LAT, dtype=jnp.int32)[:, None, None, None]
    grid_index = jnp.arange(N_GRID, dtype=jnp.int32)[None, :, None, None]
    cloud_flags = jnp.zeros((N_LAT, N_GRID, columns + 1), jnp.float32)
    cloud_flags = cloud_flags.at[lat_index, grid_index, cloud_slots].set(1.0)
    cloudy = cloud_flags[:, :, :columns].reshape(N_LAT, N_GRID, band_rows, lon_width)
    cloudy = jnp.transpose(cloudy, (0, 2, 1, 3)).reshape(nlat, nlon)
    basis_table = fourier_table(wave_order, nlon).astype(jnp.float32)
    radiation_wide = radiation.astype(jnp.float32)
    scale_factor = 1.0 / math.sqrt(nlon)
    block_rows = 8

    def row_block(first_row):
        row_strip = lax.dynamic_slice_in_dim(grid_state, first_row, block_rows, 1).astype(jnp.float32)
        flag_strip = lax.dynamic_slice_in_dim(cloudy, first_row, block_rows, 0)
        blended = jnp.einsum('fji,fg->gji', row_strip, radiation_wide)
        heating = lax.optimization_barrier((2.0 * jnp.tanh(blended)).astype(jnp.bfloat16)).astype(jnp.float32)
        heated = lax.optimization_barrier((row_strip + flag_strip[None] * heating).astype(jnp.bfloat16)).astype(jnp.float32)
        product = jnp.einsum('rml,fjl->jmrf', basis_table, heated) * scale_factor
        return product.reshape(block_rows, product.shape[1], 2 * levels).astype(jnp.bfloat16)
    starts = jnp.arange(0, nlat, block_rows, dtype=jnp.int32)
    coefs = lax.map(row_block, starts).reshape(nlat, -1, 2 * levels)
    degrees = jnp.arange(legendre.shape[2], dtype=jnp.int32)

    def one_slot(slot_index):
        column = lax.dynamic_index_in_dim(coefs, slot_index, 1, keepdims=False)
        slot_table = lax.dynamic_index_in_dim(legendre, slot_index, 0, keepdims=False)
        spectrum = jnp.dot(column.T, slot_table, preferred_element_type=jnp.float32)
        wave_number = lax.dynamic_index_in_dim(wave_order, slot_index, 0, keepdims=False)
        return jnp.where(degrees[None, :] >= wave_number, spectrum, 0.0).astype(jnp.bfloat16)
    return lax.map(one_slot, jnp.arange(wave_order.shape[0], dtype=jnp.int32))
```

```python
import math

import jax
import jax.numpy as jnp
import numpy as np
from jax import lax
from jax.sharding import PartitionSpec as P

SPARE = 24


def prolate_basis(width, waves, nlon):
    count = min(width, -(-2 * waves * width // nlon) + SPARE)
    band = (waves - 0.5) / nlon
    steps = np.arange(width, dtype=np.float64)
    centre = ((width - 1) / 2.0 - steps) ** 2 * np.cos(2.0 * np.pi * band)
    beside = steps[1:] * (width - steps[1:]) / 2.0
    system = np.diag(centre) + np.diag(beside, 1) + np.diag(beside, -1)
    _, vectors = np.linalg.eigh(system)
    leading = vectors[:, ::-1][:, :count]
    lead_sign = np.sign(np.sum(leading * (steps[:, None] + 1.0), axis=0))
    flat_sign = np.sign(np.sum(leading, axis=0))
    even = np.abs(np.sum(leading * leading[::-1], axis=0) - 1.0) < 1e-6
    return leading * np.where(even, np.where(flat_sign == 0, 1, flat_sign), np.where(lead_sign == 0, 1, lead_sign))


def fourier_table(wave_order, nlon):
    longitude = jnp.arange(nlon, dtype=jnp.int32)
    phases = wave_order[:, None] * longitude[None, :] % nlon
    angles = phases.astype(jnp.float32) * (2.0 * math.pi / nlon)
    return jnp.stack([jnp.cos(angles), -jnp.sin(angles)]).astype(jnp.bfloat16)


def cloud_mask(slots, band_rows, lon_width):
    slots = slots.reshape(-1)
    rows = (slots // lon_width)[None, :] == jnp.arange(band_rows, dtype=jnp.int32)[:, None]
    lons = (slots % lon_width)[:, None] == jnp.arange(lon_width, dtype=jnp.int32)[None, :]
    return jnp.dot(
        rows.astype(jnp.bfloat16), lons.astype(jnp.bfloat16), preferred_element_type=jnp.float32
    )


def on_device(grid_state, radiation, cloud_slots, wave_order, legendre):
    levels, band_rows, lon_width = grid_state.shape
    groups = lax.axis_size("grid")
    bands = lax.axis_size("lat")
    waves = wave_order.shape[0]
    nlon = lon_width * groups
    own_rows = band_rows // groups
    chunks = 5 if own_rows % 5 == 0 else 1
    chunk_rows = own_rows // chunks

    exact = prolate_basis(lon_width, waves, nlon)
    rank = exact.shape[1]
    compress = exact.astype(jnp.bfloat16)
    spread = exact @ np.linalg.inv(compress.astype(np.float64).T @ exact)

    mask = cloud_mask(cloud_slots, band_rows, lon_width).reshape(
        groups, own_rows, lon_width
    )
    state = grid_state.reshape(levels, groups, own_rows, lon_width)
    basis = fourier_table(wave_order, nlon).reshape(2, waves, groups, lon_width)
    expand = jnp.einsum(
        "rkgl,ln->krgn",
        basis.astype(jnp.float32),
        jnp.asarray(spread, jnp.float32),
        precision=lax.Precision.HIGHEST,
    )
    expand = (expand * (1.0 / math.sqrt(nlon))).astype(jnp.bfloat16)
    expand = expand.reshape(2 * waves, groups * rank)

    arrived = []
    for part in range(chunks):
        first = part * chunk_rows
        piece = state[:, :, first : first + chunk_rows]
        flag = mask[:, first : first + chunk_rows]
        blended = jnp.einsum("fgjl,fh->gjhl", piece, radiation, preferred_element_type=jnp.float32)
        heating = (2.0 * jnp.tanh(blended)).astype(jnp.bfloat16).astype(jnp.float32)
        heated = piece.transpose(1, 2, 0, 3).astype(jnp.float32) + heating * flag[:, :, None, :]
        packed = jnp.einsum(
            "gjhl,ln->gnjh",
            heated.astype(jnp.bfloat16),
            jnp.asarray(compress),
            preferred_element_type=jnp.float32,
        ).astype(jnp.bfloat16)
        packed = packed.reshape(groups * rank, chunk_rows * levels)
        rows = lax.all_to_all(packed, "grid", split_axis=0, concat_axis=0, tiled=True)
        coefs = jnp.dot(expand, rows, preferred_element_type=jnp.float32).astype(jnp.bfloat16)
        coefs = coefs.reshape(waves, 2, chunk_rows, levels).transpose(0, 2, 1, 3)
        coefs = coefs.reshape(waves, chunk_rows, 2 * levels)
        owned = lax.all_to_all(coefs, ("lat", "grid"), split_axis=0, concat_axis=0, tiled=True)
        arrived.append(owned.reshape(bands * groups, -1, chunk_rows, 2 * levels))

    owned_count = legendre.shape[0]
    owned = jnp.stack(arrived, axis=2).transpose(1, 0, 2, 3, 4)
    owned = owned.reshape(owned_count, bands * groups * own_rows, 2 * levels)
    position = lax.axis_index("lat") * groups + lax.axis_index("grid")
    mine = lax.dynamic_slice_in_dim(wave_order, position * owned_count, owned_count)
    spectra = jnp.einsum("kjc,kjn->kcn", owned, legendre, preferred_element_type=jnp.float32)
    degrees = jnp.arange(legendre.shape[2], dtype=jnp.int32)
    keep_mask = degrees[None, None, :] >= mine[:, None, None]
    return jnp.where(keep_mask, spectra, 0.0).astype(jnp.bfloat16)


def solution(mesh):
    in_specs = (
        P(None, "lat", "grid"),
        P(),
        P("lat", "grid", None, None),
        P(),
        P(("lat", "grid"), None, None),
    )
    out_specs = P(("lat", "grid"), None, None)
    return jax.shard_map(
        on_device, mesh=mesh, in_specs=in_specs, out_specs=out_specs, check_vma=False
    )
```

```python
import functools
import math

import jax
import jax.numpy as jnp
import numpy as np
from jax import lax
from jax.experimental import pallas as pl
from jax.experimental.pallas import tpu as pltpu
from jax.sharding import PartitionSpec as P

SPARE = 32
UNIT = 16
VMEM_BYTES = 60 * 1024 * 1024
EARLY = pl.CostEstimate(flops=1, bytes_accessed=1, transcendentals=0)
LONG = pl.CostEstimate(flops=10**12, bytes_accessed=1, transcendentals=0)
HALF_CHUNKS = (1, 1, 1, 2, 2, 1, 1, 1)


def prolate_basis(width, waves, nlon):
    count = min(width, -(-2 * waves * width // nlon) + SPARE)
    band = (waves - 0.5) / nlon
    steps = np.arange(width, dtype=np.float64)
    centre = ((width - 1) / 2.0 - steps) ** 2 * np.cos(2.0 * np.pi * band)
    beside = steps[1:] * (width - steps[1:]) / 2.0
    system = np.diag(centre) + np.diag(beside, 1) + np.diag(beside, -1)
    _, vectors = np.linalg.eigh(system)
    leading = vectors[:, ::-1][:, :count]
    lead_sign = np.sign(np.sum(leading * (steps[:, None] + 1.0), axis=0))
    flat_sign = np.sign(np.sum(leading, axis=0))
    even = np.abs(np.sum(leading * leading[::-1], axis=0) - 1.0) < 1e-6
    return leading * np.where(even, np.where(flat_sign == 0, 1, flat_sign), np.where(lead_sign == 0, 1, lead_sign))


def factor_tables(width, waves, nlon):
    exact = prolate_basis(width, waves, nlon)
    compress = exact.astype(jnp.bfloat16)
    spread = exact @ np.linalg.inv(compress.astype(np.float64).T @ exact)
    return compress, spread.astype(np.float32)


def fourier_angles(orders, longitude, nlon):
    phases = orders.reshape(2, -1, 1) * longitude % nlon
    return phases.astype(jnp.float32) * (2.0 * math.pi / nlon)


def fourier_table(wave_order, longitude, nlon):
    phases = wave_order[:, None] * longitude[None, :] % nlon
    angles = phases.astype(jnp.float32) * (2.0 * math.pi / nlon)
    return jnp.stack([jnp.cos(angles), -jnp.sin(angles)]).astype(jnp.bfloat16)


def cloud_mask(slots, band_rows, lon_width):
    slots = slots.reshape(-1)
    rows = (slots // lon_width)[None, :] == jnp.arange(band_rows, dtype=jnp.int32)[:, None]
    lons = (slots % lon_width)[:, None] == jnp.arange(lon_width, dtype=jnp.int32)[None, :]
    return jnp.dot(
        rows.astype(jnp.bfloat16), lons.astype(jnp.bfloat16), preferred_element_type=jnp.float32
    )


def params():
    return pltpu.CompilerParams(vmem_limit_bytes=VMEM_BYTES)


def later(arrays):
    return [pl.BlockSpec(memory_space=pl.ANY)] * len(arrays)


def heat_body(core_ref, state_ref, mask_ref, coupling_ref, compress_ref, *rest):
    out_ref, wide, heated = rest[-3:]
    levels = state_ref.shape[0]
    wide[...] = state_ref[...].astype(jnp.float32)
    for row in range(UNIT):
        strip = wide[:, row, :]
        blended = jnp.dot(
            coupling_ref[...], strip.astype(jnp.bfloat16), preferred_element_type=jnp.float32
        )
        heating = (2.0 * jnp.tanh(blended)).astype(jnp.bfloat16).astype(jnp.float32)
        total = strip + heating * mask_ref[row : row + 1, :]
        heated[row * levels : (row + 1) * levels, :] = total.astype(jnp.bfloat16)
    out_ref[0] = lax.dot_general(
        compress_ref[...],
        heated[...],
        (((1,), (1,)), ((), ())),
        preferred_element_type=jnp.float32,
    ).astype(jnp.bfloat16)


def heat_and_compress(core, state, mask, coupling, compress, first, units, after):
    levels, band_rows, lon_width = state.shape
    half_units = band_rows // (2 * UNIT)
    rank = compress.shape[0]

    def source(side, step, core):
        half = jnp.where(side == 0, core[0], 1 - core[0])
        return half * half_units + first + step

    block = UNIT * levels
    return pl.pallas_call(
        heat_body,
        grid_spec=pltpu.PrefetchScalarGridSpec(
            num_scalar_prefetch=1,
            grid=(2, units),
            in_specs=[
                pl.BlockSpec((levels, UNIT, lon_width), lambda a, b, c: (0, source(a, b, c), 0)),
                pl.BlockSpec((UNIT, lon_width), lambda a, b, c: (source(a, b, c), 0)),
                pl.BlockSpec((levels, levels), lambda a, b, c: (0, 0)),
                pl.BlockSpec((rank, lon_width), lambda a, b, c: (0, 0)),
            ]
            + later(after),
            out_specs=pl.BlockSpec((1, rank, block), lambda a, b, c: (a, 0, b)),
            scratch_shapes=[
                pltpu.VMEM((levels, UNIT, lon_width), jnp.float32),
                pltpu.VMEM((block, lon_width), jnp.bfloat16),
            ],
        ),
        out_shape=jax.ShapeDtypeStruct((2, rank, units * block), jnp.bfloat16),
        compiler_params=params(),
        cost_estimate=EARLY,
    )(core, state, mask, coupling, compress, *after)


def join_body(core_ref, mine_ref, arrived_ref, *rest):
    out_ref = rest[-1]
    out_ref[0] = jnp.where(core_ref[0] == pl.program_id(0), mine_ref[0], arrived_ref[...])


def join_cores(core, both, arrived, after):
    _, rank, lanes = both.shape
    return pl.pallas_call(
        join_body,
        grid_spec=pltpu.PrefetchScalarGridSpec(
            num_scalar_prefetch=1,
            grid=(2,),
            in_specs=[
                pl.BlockSpec((1, rank, lanes), lambda a, c: (0, 0, 0)),
                pl.BlockSpec((rank, lanes), lambda a, c: (0, 0)),
            ]
            + later(after),
            out_specs=pl.BlockSpec((1, rank, lanes), lambda a, c: (a, 0, 0)),
        ),
        out_shape=jax.ShapeDtypeStruct(both.shape, jnp.bfloat16),
        compiler_params=params(),
        cost_estimate=EARLY,
    )(core, both, arrived, *after)


def choose_body(inner_ref, near_ref, away_ref, *rest):
    out_ref = rest[-1]
    out_ref[...] = jnp.where(inner_ref[0] == 1, near_ref[...], away_ref[...])


def choose(inner, near, away, after):
    slots, rows, columns = near.shape
    step = slots // 4
    spec = pl.BlockSpec((step, rows, columns), lambda k, c: (k, 0, 0))
    return pl.pallas_call(
        choose_body,
        grid_spec=pltpu.PrefetchScalarGridSpec(
            num_scalar_prefetch=1,
            grid=(4,),
            in_specs=[spec, spec] + later(after),
            out_specs=spec,
        ),
        out_shape=jax.ShapeDtypeStruct(near.shape, jnp.bfloat16),
        compiler_params=params(),
        cost_estimate=EARLY,
    )(inner, near, away, *after)


def stack_pieces(a_ref, b_ref):
    rank, lanes = a_ref.shape[1:]
    return jnp.concatenate(
        [a_ref[...].reshape(2 * rank, lanes), b_ref[...].reshape(2 * rank, lanes)], axis=0
    )


def partial_body(expand_ref, a_ref, b_ref, *rest):
    out_ref = rest[-1]
    rows = stack_pieces(a_ref, b_ref)
    for part in range(expand_ref.shape[0]):
        out_ref[part] = jnp.dot(expand_ref[part], rows, preferred_element_type=jnp.float32).astype(
            jnp.bfloat16
        )


def partial_sums(expand, pieces, block, after):
    _, rank, lanes = pieces[0].shape
    parts, waves, _ = expand.shape
    return pl.pallas_call(
        partial_body,
        grid=(lanes // block,),
        in_specs=[pl.BlockSpec(expand.shape, lambda i: (0, 0, 0))]
        + [pl.BlockSpec((2, rank, block), lambda i: (0, 0, i))] * 2
        + later(after),
        out_specs=pl.BlockSpec((parts, waves, block), lambda i: (0, 0, i)),
        out_shape=jax.ShapeDtypeStruct((parts, waves, lanes), jnp.bfloat16),
        compiler_params=params(),
        cost_estimate=EARLY,
    )(expand, *pieces, *after)


def total_body(levels, expand_ref, a_ref, b_ref, far_ref, *rest):
    parts = expand_ref.shape[0]
    outs, total, laid = rest[-2 - parts : -2], rest[-2], rest[-1]
    rows = stack_pieces(a_ref, b_ref)
    slots = total.shape[0] // 2
    for part, out in enumerate(outs):
        total[...] = jnp.dot(
            expand_ref[part], rows, preferred_element_type=jnp.float32
        ) + far_ref[part].astype(jnp.float32)
        for row in range(UNIT):
            lanes = slice(row * levels, (row + 1) * levels)
            laid[:, row, :] = jnp.concatenate([total[:slots, lanes], total[slots:, lanes]], axis=1)
        out[...] = laid[...].astype(jnp.bfloat16)


def total_sums(expand, pieces, far, levels, after, weight):
    _, rank, lanes = pieces[0].shape
    parts, waves, _ = expand.shape
    block = UNIT * levels
    slots = waves // 2
    units = lanes // block
    shape = jax.ShapeDtypeStruct((slots, units * UNIT, 2 * levels), jnp.bfloat16)
    return pl.pallas_call(
        functools.partial(total_body, levels),
        grid=(units,),
        in_specs=[pl.BlockSpec(expand.shape, lambda i: (0, 0, 0))]
        + [pl.BlockSpec((2, rank, block), lambda i: (0, 0, i))] * 2
        + [pl.BlockSpec((parts, waves, block), lambda i: (0, 0, i))]
        + later(after),
        out_specs=[pl.BlockSpec((slots, UNIT, 2 * levels), lambda i: (0, i, 0))] * parts,
        out_shape=[shape] * parts,
        scratch_shapes=[
            pltpu.VMEM((waves, block), jnp.float32),
            pltpu.VMEM((slots, UNIT, 2 * levels), jnp.float32),
        ],
        compiler_params=params(),
        cost_estimate=weight,
    )(expand, *pieces, far, *after)


def gather_rows(parts, starts, half_rows, column):
    for part, start in zip(parts, starts):
        rows = part.shape[3]
        for side in range(part.shape[0] * 2):
            first = side * half_rows + start
            column[first : first + rows, :] = part[side // 2, side % 2, 0]


def legendre_body(starts, half_rows, stop, legendre_ref, *rest):
    parts, out_ref, column, table = rest[: len(starts)], rest[-3], rest[-2], rest[-1]
    gather_rows(parts, starts, stop, column)
    for side in range(column.shape[0] // stop):
        table[side * stop : (side + 1) * stop] = legendre_ref[0, side * half_rows : side * half_rows + stop]
    out_ref[0] = lax.dot_general(
        column[...], table[...], (((0,), (0,)), ((), ())), preferred_element_type=jnp.float32
    )


def slot_blocks(parts):
    return [
        pl.BlockSpec((part.shape[0], 2, 1) + part.shape[3:], lambda k, *_: (0, 0, k, 0, 0)) for part in parts
    ]


def legendre_start(legendre, parts, starts, half_rows, after):
    owned_count, nlat, degrees = legendre.shape
    columns = parts[0].shape[-1]
    stop = starts[-1] + parts[-1].shape[3]
    kept = nlat // half_rows * stop
    return pl.pallas_call(
        functools.partial(legendre_body, starts, half_rows, stop),
        grid=(owned_count,),
        in_specs=[pl.BlockSpec((1, nlat, degrees), lambda k: (k, 0, 0))] + slot_blocks(parts) + later(after),
        out_specs=pl.BlockSpec((1, columns, degrees), lambda k: (k, 0, 0)),
        scratch_shapes=[pltpu.VMEM((kept, columns), jnp.bfloat16), pltpu.VMEM((kept, degrees), jnp.bfloat16)],
        out_shape=jax.ShapeDtypeStruct((owned_count, columns, degrees), jnp.float32),
        compiler_params=params(),
        cost_estimate=EARLY,
    )(legendre, *parts, *after)


def legendre_rest_body(starts, mine_ref, legendre_ref, so_far_ref, *rest):
    parts, out_ref, column, table = rest[: len(starts)], rest[-3], rest[-2], rest[-1]
    rows = legendre_ref.shape[2]
    gather_rows(parts, starts, rows, column)
    for side in range(legendre_ref.shape[1]):
        table[side * rows : (side + 1) * rows] = legendre_ref[0, side]
    spectrum = so_far_ref[0] + lax.dot_general(
        column[...], table[...], (((0,), (0,)), ((), ())), preferred_element_type=jnp.float32
    )
    degrees = lax.broadcasted_iota(jnp.int32, spectrum.shape, 1)
    wave = mine_ref[pl.program_id(0)]
    out_ref[0] = jnp.where(degrees >= wave, spectrum, 0.0).astype(jnp.bfloat16)


def legendre_rest(mine, legendre, parts, starts, half_rows, so_far):
    owned_count, nlat, degrees = legendre.shape
    columns = parts[0].shape[-1]
    rows = half_rows - starts[0]
    sides = nlat // half_rows
    starts = [start - starts[0] for start in starts]
    return pl.pallas_call(
        functools.partial(legendre_rest_body, starts),
        grid_spec=pltpu.PrefetchScalarGridSpec(
            num_scalar_prefetch=1,
            grid=(owned_count,),
            in_specs=[
                pl.BlockSpec((1, sides, rows, degrees), lambda k, m: (k, 0, half_rows // rows - 1, 0)),
                pl.BlockSpec((1, columns, degrees), lambda k, m: (k, 0, 0)),
            ]
            + slot_blocks(parts),
            out_specs=pl.BlockSpec((1, columns, degrees), lambda k, m: (k, 0, 0)),
            scratch_shapes=[
                pltpu.VMEM((sides * rows, columns), jnp.bfloat16),
                pltpu.VMEM((sides * rows, degrees), jnp.bfloat16),
            ],
        ),
        out_shape=jax.ShapeDtypeStruct((owned_count, columns, degrees), jnp.bfloat16),
        compiler_params=params(),
        cost_estimate=EARLY,
    )(mine, legendre.reshape(owned_count, sides, half_rows, degrees), so_far, *parts)


def on_line(grid_state, radiation, cloud_slots, wave_order, legendre):
    levels, band_rows, lon_width = grid_state.shape
    groups = lax.axis_size("grid")
    bands = lax.axis_size("lat")
    waves = wave_order.shape[0]
    nlon = lon_width * groups
    half_rows = band_rows // 2
    owned_count = legendre.shape[0]
    here = lax.axis_index("grid")
    core, chip = here % 2, here // 2
    side = chip // 2
    is_inner = (chip == 1) | (chip == 2)
    inner_chip = jnp.where(side == 0, 1, 2)
    outer_chip = jnp.where(side == 0, 0, 3)

    compress, spread = factor_tables(lon_width, waves, nlon)
    rank = compress.shape[1]
    compress = jnp.asarray(np.ascontiguousarray(compress.T))
    mask = cloud_mask(cloud_slots, band_rows, lon_width)
    coupling = radiation.T
    core_ref = core.astype(jnp.int32).reshape(1)
    inner_ref = is_inner.astype(jnp.int32).reshape(1)

    chips = jnp.stack([inner_chip, outer_chip])
    sources = (2 * chips[:, None] + jnp.arange(2, dtype=jnp.int32)).reshape(-1)

    def slots_of(chips):
        device = (
            jnp.arange(bands, dtype=jnp.int32)[None, :, None] * groups
            + 2 * chips[:, None, None]
            + jnp.arange(2, dtype=jnp.int32)
        )
        slot = device[..., None] * owned_count + jnp.arange(owned_count, dtype=jnp.int32)
        return slot.reshape(-1)

    def expand_for(slots):
        order = wave_order[slots]
        near = fourier_angles(order, jnp.arange(lon_width, dtype=jnp.int32), nlon)[:, :, None, :]
        turn = fourier_angles(order, sources * lon_width, nlon)[:, :, :, None]
        basis = jnp.stack(
            [
                jnp.cos(near) * jnp.cos(turn) - jnp.sin(near) * jnp.sin(turn),
                -(jnp.sin(near) * jnp.cos(turn) + jnp.cos(near) * jnp.sin(turn)),
            ],
            axis=1,
        ).astype(jnp.bfloat16)
        table = jnp.einsum(
            "prkgl,ln->prkgn",
            basis.astype(jnp.float32),
            jnp.asarray(spread),
            precision=lax.Precision.HIGHEST,
        )
        table = (table * (1.0 / math.sqrt(nlon))).astype(jnp.bfloat16)
        return table.reshape(2, slots.shape[0], 4 * rank)

    expand_far = expand_for(slots_of(3 - chips))
    expand_near = expand_for(slots_of(chips))

    to_inner = [(0, 2), (1, 3), (6, 4), (7, 5)]
    across = [(2, 4), (3, 5), (4, 2), (5, 3)]
    to_outer = [(2, 0), (3, 1), (4, 6), (5, 7)]
    beside = [(i, i ^ 1) for i in range(groups)]

    plane = [
        [band * groups + 2 * here + core for band in range(bands) for core in range(2)]
        for here in range(groups // 2)
    ]

    count = len(HALF_CHUNKS)
    starts = [sum(HALF_CHUNKS[:i]) for i in range(count)]
    halves, pieces, sums, totals, owned = {}, {}, {}, {}, {}
    last = [expand_far]

    def heat(i):
        halves[i] = heat_and_compress(
            core_ref, grid_state, mask, coupling, compress, starts[i], HALF_CHUNKS[i], last if i else []
        )
        if i:
            last[:] = [halves[i]]

    def join(i):
        arrived = lax.ppermute(halves[i][1], "grid", beside)
        joined = join_cores(core_ref, halves[i], arrived, last)
        pieces[i] = [joined, lax.ppermute(joined, "grid", to_inner)]
        last[:] = [joined]

    def send(i, part):
        expand = expand_far if part is None else expand_far[part : part + 1]
        sums[i, part] = partial_sums(expand, pieces[i], UNIT * levels, last)
        last[:] = [sums[i, part]]

    def add(i, part):
        expand = expand_near if part is None else expand_near[part : part + 1]
        far = lax.ppermute(sums[i, part], "grid", across)
        found = total_sums(expand, pieces[i], far, levels, last, LONG if i else EARLY)
        if part is None:
            totals[i, 0], totals[i, 1] = found
        else:
            totals[i, part] = found[0]
        last[:] = [found[0]]

    def share(i):
        away = lax.ppermute(totals[i, 1], "grid", to_outer)
        after = last + ([owned[i - 1]] if 0 < i < final else [])
        laid = choose(inner_ref, totals[i, 0], away, after)
        last[:] = [laid]
        owned[i] = lax.all_to_all(
            laid, ("lat", "grid"), split_axis=0, concat_axis=0, axis_index_groups=plane, tiled=True
        ).reshape((bands, 2, owned_count) + laid.shape[1:])

    final = count - 1
    rows = [UNIT * i for i in starts]
    heat(0)
    join(0)
    heat(1)
    heat(2)
    join(1)
    join(2)
    send(0, None)
    heat(3)
    send(1, None)
    join(3)
    for i in range(final):
        add(i, None)
        if i + 3 < count and i > 0:
            join(i + 3)
        if i + 4 < count:
            heat(i + 4)
        if i > 0:
            share(i - 1)
        if i + 2 < final:
            send(i + 2, None)
        elif i + 2 == final:
            send(final, 1)
            send(final, 0)
    add(final, 1)
    share(final - 1)
    add(final, 0)
    share(final)
    so_far = legendre_start(legendre, [owned[k] for k in range(final)], rows[:final], half_rows, last)

    position = lax.axis_index("lat") * groups + here
    taken = lax.dynamic_slice_in_dim(wave_order, position * owned_count, owned_count)
    return legendre_rest(taken, legendre, [owned[final]], rows[final:], half_rows, so_far)


def on_device(grid_state, radiation, cloud_slots, wave_order, legendre):
    levels, band_rows, lon_width = grid_state.shape
    groups = lax.axis_size("grid")
    bands = lax.axis_size("lat")
    waves = wave_order.shape[0]
    nlon = lon_width * groups
    own_rows = band_rows // groups
    chunks = 5 if own_rows % 5 == 0 else 1
    chunk_rows = own_rows // chunks

    compress, spread = factor_tables(lon_width, waves, nlon)
    rank = compress.shape[1]
    mask = cloud_mask(cloud_slots, band_rows, lon_width).reshape(groups, own_rows, lon_width)
    state = grid_state.reshape(levels, groups, own_rows, lon_width)
    basis = fourier_table(wave_order, jnp.arange(nlon, dtype=jnp.int32), nlon)
    expand = jnp.einsum(
        "rkgl,ln->krgn",
        basis.reshape(2, waves, groups, lon_width).astype(jnp.float32),
        jnp.asarray(spread),
        precision=lax.Precision.HIGHEST,
    )
    expand = (expand * (1.0 / math.sqrt(nlon))).astype(jnp.bfloat16)
    expand = expand.reshape(2 * waves, groups * rank)

    arrived = []
    for part in range(chunks):
        first = part * chunk_rows
        piece = state[:, :, first : first + chunk_rows]
        flag = mask[:, first : first + chunk_rows]
        blended = jnp.einsum("fgjl,fh->gjhl", piece, radiation, preferred_element_type=jnp.float32)
        heating = (2.0 * jnp.tanh(blended)).astype(jnp.bfloat16).astype(jnp.float32)
        heated = piece.transpose(1, 2, 0, 3).astype(jnp.float32) + heating * flag[:, :, None, :]
        packed = jnp.einsum(
            "gjhl,ln->gnjh",
            heated.astype(jnp.bfloat16),
            jnp.asarray(compress),
            preferred_element_type=jnp.float32,
        ).astype(jnp.bfloat16)
        packed = packed.reshape(groups * rank, chunk_rows * levels)
        rows = lax.all_to_all(packed, "grid", split_axis=0, concat_axis=0, tiled=True)
        coefs = jnp.dot(expand, rows, preferred_element_type=jnp.float32).astype(jnp.bfloat16)
        coefs = coefs.reshape(waves, 2, chunk_rows, levels).transpose(0, 2, 1, 3)
        coefs = coefs.reshape(waves, chunk_rows, 2 * levels)
        owned = lax.all_to_all(coefs, ("lat", "grid"), split_axis=0, concat_axis=0, tiled=True)
        arrived.append(owned.reshape(bands * groups, -1, chunk_rows, 2 * levels))

    owned_count = legendre.shape[0]
    owned = jnp.stack(arrived, axis=2).transpose(1, 0, 2, 3, 4)
    owned = owned.reshape(owned_count, bands * groups * own_rows, 2 * levels)
    position = lax.axis_index("lat") * groups + lax.axis_index("grid")
    mine = lax.dynamic_slice_in_dim(wave_order, position * owned_count, owned_count)
    spectra = jnp.einsum("kjc,kjn->kcn", owned, legendre, preferred_element_type=jnp.float32)
    degrees = jnp.arange(legendre.shape[2], dtype=jnp.int32)
    keep_mask = degrees[None, None, :] >= mine[:, None, None]
    return jnp.where(keep_mask, spectra, 0.0).astype(jnp.bfloat16)


def solution(mesh):
    in_specs = (
        P(None, "lat", "grid"),
        P(),
        P("lat", "grid", None, None),
        P(),
        P(("lat", "grid"), None, None),
    )
    out_specs = P(("lat", "grid"), None, None)

    def local(grid_state, radiation, cloud_slots, wave_order, legendre):
        half_units = sum(HALF_CHUNKS)
        fits = mesh.shape["grid"] == 8 and grid_state.shape[1] == 2 * UNIT * half_units
        program = on_line if fits else on_device
        return program(grid_state, radiation, cloud_slots, wave_order, legendre)

    return jax.shard_map(
        local, mesh=mesh, in_specs=in_specs, out_specs=out_specs, check_vma=False
    )
```

```python
import functools
import math

import jax
import jax.numpy as jnp
import numpy as np
from jax import lax
from jax.experimental import pallas as pl
from jax.experimental.pallas import tpu as pltpu
from jax.sharding import PartitionSpec as P

SPARE = 32
UNIT = 16
VMEM_BYTES = 60 * 1024 * 1024
EARLY = pl.CostEstimate(flops=1, bytes_accessed=1, transcendentals=0)
LONG = pl.CostEstimate(flops=10**12, bytes_accessed=1, transcendentals=0)
HALF_CHUNKS = (1, 1, 1, 2, 2, 1, 1, 1)


def prolate_basis(width, waves, nlon):
    count = min(width, -(-2 * waves * width // nlon) + SPARE)
    band = (waves - 0.5) / nlon
    steps = np.arange(width, dtype=np.float64)
    centre = ((width - 1) / 2.0 - steps) ** 2 * np.cos(2.0 * np.pi * band)
    beside = steps[1:] * (width - steps[1:]) / 2.0
    system = np.diag(centre) + np.diag(beside, 1) + np.diag(beside, -1)
    _, vectors = np.linalg.eigh(system)
    leading = vectors[:, ::-1][:, :count]
    lead_sign = np.sign(np.sum(leading * (steps[:, None] + 1.0), axis=0))
    flat_sign = np.sign(np.sum(leading, axis=0))
    even = np.abs(np.sum(leading * leading[::-1], axis=0) - 1.0) < 1e-6
    return leading * np.where(even, np.where(flat_sign == 0, 1, flat_sign), np.where(lead_sign == 0, 1, lead_sign))


def factor_tables(width, waves, nlon):
    exact = prolate_basis(width, waves, nlon)
    compress = exact.astype(jnp.bfloat16)
    spread = exact @ np.linalg.inv(compress.astype(np.float64).T @ exact)
    return compress, spread.astype(np.float32)


def fourier_angles(orders, longitude, nlon):
    phases = orders.reshape(2, -1, 1) * longitude % nlon
    return phases.astype(jnp.float32) * (2.0 * math.pi / nlon)


def fourier_table(wave_order, longitude, nlon):
    phases = wave_order[:, None] * longitude[None, :] % nlon
    angles = phases.astype(jnp.float32) * (2.0 * math.pi / nlon)
    return jnp.stack([jnp.cos(angles), -jnp.sin(angles)]).astype(jnp.bfloat16)


def cloud_mask(slots, band_rows, lon_width):
    slots = slots.reshape(-1)
    rows = (slots // lon_width)[None, :] == jnp.arange(band_rows, dtype=jnp.int32)[:, None]
    lons = (slots % lon_width)[:, None] == jnp.arange(lon_width, dtype=jnp.int32)[None, :]
    return jnp.dot(
        rows.astype(jnp.bfloat16), lons.astype(jnp.bfloat16), preferred_element_type=jnp.float32
    )


def params():
    return pltpu.CompilerParams(vmem_limit_bytes=VMEM_BYTES)


def later(arrays):
    return [pl.BlockSpec(memory_space=pl.ANY)] * len(arrays)


def heat_body(core_ref, state_ref, mask_ref, coupling_ref, compress_ref, *rest):
    out_ref, wide, heated = rest[-3:]
    levels = state_ref.shape[0]
    wide[...] = state_ref[...].astype(jnp.float32)
    for row in range(UNIT):
        strip = wide[:, row, :]
        blended = jnp.dot(
            coupling_ref[...], strip.astype(jnp.bfloat16), preferred_element_type=jnp.float32
        )
        heating = (2.0 * jnp.tanh(blended)).astype(jnp.bfloat16).astype(jnp.float32)
        total = strip + heating * mask_ref[row : row + 1, :]
        heated[row * levels : (row + 1) * levels, :] = total.astype(jnp.bfloat16)
    out_ref[0] = lax.dot_general(
        compress_ref[...],
        heated[...],
        (((1,), (1,)), ((), ())),
        preferred_element_type=jnp.float32,
    ).astype(jnp.bfloat16)


def heat_and_compress(core, state, mask, coupling, compress, first, units, after):
    levels, band_rows, lon_width = state.shape
    half_units = band_rows // (2 * UNIT)
    rank = compress.shape[0]

    def source(side, step, core):
        half = jnp.where(side == 0, core[0], 1 - core[0])
        return half * half_units + first + step

    block = UNIT * levels
    return pl.pallas_call(
        heat_body,
        grid_spec=pltpu.PrefetchScalarGridSpec(
            num_scalar_prefetch=1,
            grid=(2, units),
            in_specs=[
                pl.BlockSpec((levels, UNIT, lon_width), lambda a, b, c: (0, source(a, b, c), 0)),
                pl.BlockSpec((UNIT, lon_width), lambda a, b, c: (source(a, b, c), 0)),
                pl.BlockSpec((levels, levels), lambda a, b, c: (0, 0)),
                pl.BlockSpec((rank, lon_width), lambda a, b, c: (0, 0)),
            ]
            + later(after),
            out_specs=pl.BlockSpec((1, rank, block), lambda a, b, c: (a, 0, b)),
            scratch_shapes=[
                pltpu.VMEM((levels, UNIT, lon_width), jnp.float32),
                pltpu.VMEM((block, lon_width), jnp.bfloat16),
            ],
        ),
        out_shape=jax.ShapeDtypeStruct((2, rank, units * block), jnp.bfloat16),
        compiler_params=params(),
        cost_estimate=EARLY,
    )(core, state, mask, coupling, compress, *after)


def join_body(core_ref, mine_ref, arrived_ref, *rest):
    out_ref = rest[-1]
    out_ref[0] = jnp.where(core_ref[0] == pl.program_id(0), mine_ref[0], arrived_ref[...])


def join_cores(core, both, arrived, after):
    _, rank, lanes = both.shape
    return pl.pallas_call(
        join_body,
        grid_spec=pltpu.PrefetchScalarGridSpec(
            num_scalar_prefetch=1,
            grid=(2,),
            in_specs=[
                pl.BlockSpec((1, rank, lanes), lambda a, c: (0, 0, 0)),
                pl.BlockSpec((rank, lanes), lambda a, c: (0, 0)),
            ]
            + later(after),
            out_specs=pl.BlockSpec((1, rank, lanes), lambda a, c: (a, 0, 0)),
        ),
        out_shape=jax.ShapeDtypeStruct(both.shape, jnp.bfloat16),
        compiler_params=params(),
        cost_estimate=EARLY,
    )(core, both, arrived, *after)


def choose_body(inner_ref, near_ref, away_ref, *rest):
    out_ref = rest[-1]
    out_ref[...] = jnp.where(inner_ref[0] == 1, near_ref[...], away_ref[...])


def choose(inner, near, away, after):
    slots, rows, columns = near.shape
    step = slots // 4
    spec = pl.BlockSpec((step, rows, columns), lambda k, c: (k, 0, 0))
    return pl.pallas_call(
        choose_body,
        grid_spec=pltpu.PrefetchScalarGridSpec(
            num_scalar_prefetch=1,
            grid=(4,),
            in_specs=[spec, spec] + later(after),
            out_specs=spec,
        ),
        out_shape=jax.ShapeDtypeStruct(near.shape, jnp.bfloat16),
        compiler_params=params(),
        cost_estimate=EARLY,
    )(inner, near, away, *after)


def stack_pieces(a_ref, b_ref):
    rank, lanes = a_ref.shape[1:]
    return jnp.concatenate(
        [a_ref[...].reshape(2 * rank, lanes), b_ref[...].reshape(2 * rank, lanes)], axis=0
    )


def partial_body(expand_ref, a_ref, b_ref, *rest):
    out_ref = rest[-1]
    rows = stack_pieces(a_ref, b_ref)
    for part in range(expand_ref.shape[0]):
        out_ref[part] = jnp.dot(expand_ref[part], rows, preferred_element_type=jnp.float32).astype(
            jnp.bfloat16
        )


def partial_sums(expand, pieces, block, after):
    _, rank, lanes = pieces[0].shape
    parts, waves, _ = expand.shape
    return pl.pallas_call(
        partial_body,
        grid=(lanes // block,),
        in_specs=[pl.BlockSpec(expand.shape, lambda i: (0, 0, 0))]
        + [pl.BlockSpec((2, rank, block), lambda i: (0, 0, i))] * 2
        + later(after),
        out_specs=pl.BlockSpec((parts, waves, block), lambda i: (0, 0, i)),
        out_shape=jax.ShapeDtypeStruct((parts, waves, lanes), jnp.bfloat16),
        compiler_params=params(),
        cost_estimate=EARLY,
    )(expand, *pieces, *after)


def total_body(levels, expand_ref, a_ref, b_ref, far_ref, *rest):
    parts = expand_ref.shape[0]
    outs, total, laid = rest[-2 - parts : -2], rest[-2], rest[-1]
    rows = stack_pieces(a_ref, b_ref)
    slots = total.shape[0] // 2
    for part, out in enumerate(outs):
        total[...] = jnp.dot(
            expand_ref[part], rows, preferred_element_type=jnp.float32
        ) + far_ref[part].astype(jnp.float32)
        for row in range(UNIT):
            lanes = slice(row * levels, (row + 1) * levels)
            laid[:, row, :] = jnp.concatenate([total[:slots, lanes], total[slots:, lanes]], axis=1)
        out[...] = laid[...].astype(jnp.bfloat16)


def total_sums(expand, pieces, far, levels, after, weight):
    _, rank, lanes = pieces[0].shape
    parts, waves, _ = expand.shape
    block = UNIT * levels
    slots = waves // 2
    units = lanes // block
    shape = jax.ShapeDtypeStruct((slots, units * UNIT, 2 * levels), jnp.bfloat16)
    return pl.pallas_call(
        functools.partial(total_body, levels),
        grid=(units,),
        in_specs=[pl.BlockSpec(expand.shape, lambda i: (0, 0, 0))]
        + [pl.BlockSpec((2, rank, block), lambda i: (0, 0, i))] * 2
        + [pl.BlockSpec((parts, waves, block), lambda i: (0, 0, i))]
        + later(after),
        out_specs=[pl.BlockSpec((slots, UNIT, 2 * levels), lambda i: (0, i, 0))] * parts,
        out_shape=[shape] * parts,
        scratch_shapes=[
            pltpu.VMEM((waves, block), jnp.float32),
            pltpu.VMEM((slots, UNIT, 2 * levels), jnp.float32),
        ],
        compiler_params=params(),
        cost_estimate=weight,
    )(expand, *pieces, far, *after)


def gather_rows(parts, starts, half_rows, column, slot=0):
    for part, start in zip(parts, starts):
        rows = part.shape[3]
        for side in range(part.shape[0] * 2):
            first = side * half_rows + start
            column[first : first + rows, :] = part[side // 2, side % 2, slot]


def legendre_body(starts, half_rows, stop, legendre_ref, *rest):
    parts, out_ref, column, table = rest[: len(starts)], rest[-3], rest[-2], rest[-1]
    gather_rows(parts, starts, stop, column)
    for side in range(column.shape[0] // stop):
        table[side * stop : (side + 1) * stop] = legendre_ref[0, side * half_rows : side * half_rows + stop]
    out_ref[0] = lax.dot_general(
        column[...], table[...], (((0,), (0,)), ((), ())), preferred_element_type=jnp.float32
    )


def slot_blocks(parts, group=1):
    return [
        pl.BlockSpec((part.shape[0], 2, group) + part.shape[3:], lambda k, *_: (0, 0, k, 0, 0))
        for part in parts
    ]


def legendre_start(legendre, parts, starts, half_rows, after):
    owned_count, nlat, degrees = legendre.shape
    columns = parts[0].shape[-1]
    stop = starts[-1] + parts[-1].shape[3]
    kept = nlat // half_rows * stop
    return pl.pallas_call(
        functools.partial(legendre_body, starts, half_rows, stop),
        grid=(owned_count,),
        in_specs=[pl.BlockSpec((1, nlat, degrees), lambda k: (k, 0, 0))] + slot_blocks(parts) + later(after),
        out_specs=pl.BlockSpec((1, columns, degrees), lambda k: (k, 0, 0)),
        scratch_shapes=[pltpu.VMEM((kept, columns), jnp.bfloat16), pltpu.VMEM((kept, degrees), jnp.bfloat16)],
        out_shape=jax.ShapeDtypeStruct((owned_count, columns, degrees), jnp.float32),
        compiler_params=params(),
        cost_estimate=EARLY,
    )(legendre, *parts, *after)


def legendre_rest_body(starts, mine_ref, legendre_ref, so_far_ref, *rest):
    parts, out_ref, column, table = rest[: len(starts)], rest[-3], rest[-2], rest[-1]
    rows = legendre_ref.shape[2]
    group = out_ref.shape[0]
    for slot in range(group):
        gather_rows(parts, starts, rows, column, slot)
        for side in range(legendre_ref.shape[1]):
            table[side * rows : (side + 1) * rows] = legendre_ref[slot, side]
        spectrum = so_far_ref[slot] + lax.dot_general(
            column[...], table[...], (((0,), (0,)), ((), ())), preferred_element_type=jnp.float32
        )
        degrees = lax.broadcasted_iota(jnp.int32, spectrum.shape, 1)
        wave = mine_ref[pl.program_id(0) * group + slot]
        out_ref[slot] = jnp.where(degrees >= wave, spectrum, 0.0).astype(jnp.bfloat16)


def legendre_rest(mine, legendre, parts, starts, half_rows, so_far):
    owned_count, nlat, degrees = legendre.shape
    columns = parts[0].shape[-1]
    rows = half_rows - starts[0]
    sides = nlat // half_rows
    starts = [start - starts[0] for start in starts]
    group = 2 if owned_count % 2 == 0 else 1
    return pl.pallas_call(
        functools.partial(legendre_rest_body, starts),
        grid_spec=pltpu.PrefetchScalarGridSpec(
            num_scalar_prefetch=1,
            grid=(owned_count // group,),
            in_specs=[
                pl.BlockSpec((group, sides, rows, degrees), lambda k, m: (k, 0, half_rows // rows - 1, 0)),
                pl.BlockSpec((group, columns, degrees), lambda k, m: (k, 0, 0)),
            ]
            + slot_blocks(parts, group),
            out_specs=pl.BlockSpec((group, columns, degrees), lambda k, m: (k, 0, 0)),
            scratch_shapes=[
                pltpu.VMEM((sides * rows, columns), jnp.bfloat16),
                pltpu.VMEM((sides * rows, degrees), jnp.bfloat16),
            ],
        ),
        out_shape=jax.ShapeDtypeStruct((owned_count, columns, degrees), jnp.bfloat16),
        compiler_params=params(),
        cost_estimate=EARLY,
    )(mine, legendre.reshape(owned_count, sides, half_rows, degrees), so_far, *parts)


def on_line(grid_state, radiation, cloud_slots, wave_order, legendre):
    levels, band_rows, lon_width = grid_state.shape
    groups = lax.axis_size("grid")
    bands = lax.axis_size("lat")
    waves = wave_order.shape[0]
    nlon = lon_width * groups
    half_rows = band_rows // 2
    owned_count = legendre.shape[0]
    here = lax.axis_index("grid")
    core, chip = here % 2, here // 2
    side = chip // 2
    is_inner = (chip == 1) | (chip == 2)
    inner_chip = jnp.where(side == 0, 1, 2)
    outer_chip = jnp.where(side == 0, 0, 3)

    compress, spread = factor_tables(lon_width, waves, nlon)
    rank = compress.shape[1]
    compress = jnp.asarray(np.ascontiguousarray(compress.T))
    mask = cloud_mask(cloud_slots, band_rows, lon_width)
    coupling = radiation.T
    core_ref = core.astype(jnp.int32).reshape(1)
    inner_ref = is_inner.astype(jnp.int32).reshape(1)

    chips = jnp.stack([inner_chip, outer_chip])
    sources = (2 * chips[:, None] + jnp.arange(2, dtype=jnp.int32)).reshape(-1)

    def slots_of(chips):
        device = (
            jnp.arange(bands, dtype=jnp.int32)[None, :, None] * groups
            + 2 * chips[:, None, None]
            + jnp.arange(2, dtype=jnp.int32)
        )
        slot = device[..., None] * owned_count + jnp.arange(owned_count, dtype=jnp.int32)
        return slot.reshape(-1)

    def expand_for(slots):
        order = wave_order[slots]
        near = fourier_angles(order, jnp.arange(lon_width, dtype=jnp.int32), nlon)[:, :, None, :]
        turn = fourier_angles(order, sources * lon_width, nlon)[:, :, :, None]
        basis = jnp.stack(
            [
                jnp.cos(near) * jnp.cos(turn) - jnp.sin(near) * jnp.sin(turn),
                -(jnp.sin(near) * jnp.cos(turn) + jnp.cos(near) * jnp.sin(turn)),
            ],
            axis=1,
        ).astype(jnp.bfloat16)
        table = jnp.einsum(
            "prkgl,ln->prkgn",
            basis.astype(jnp.float32),
            jnp.asarray(spread),
            precision=lax.Precision.HIGHEST,
        )
        table = (table * (1.0 / math.sqrt(nlon))).astype(jnp.bfloat16)
        return table.reshape(2, slots.shape[0], 4 * rank)

    expand_far = expand_for(slots_of(3 - chips))
    expand_near = expand_for(slots_of(chips))

    to_inner = [(0, 2), (1, 3), (6, 4), (7, 5)]
    across = [(2, 4), (3, 5), (4, 2), (5, 3)]
    to_outer = [(2, 0), (3, 1), (4, 6), (5, 7)]
    beside = [(i, i ^ 1) for i in range(groups)]

    plane = [
        [band * groups + 2 * here + core for band in range(bands) for core in range(2)]
        for here in range(groups // 2)
    ]

    count = len(HALF_CHUNKS)
    starts = [sum(HALF_CHUNKS[:i]) for i in range(count)]
    halves, pieces, sums, totals, owned = {}, {}, {}, {}, {}
    last = [expand_far]

    def heat(i):
        halves[i] = heat_and_compress(
            core_ref, grid_state, mask, coupling, compress, starts[i], HALF_CHUNKS[i], last if i else []
        )
        if i:
            last[:] = [halves[i]]

    def join(i):
        arrived = lax.ppermute(halves[i][1], "grid", beside)
        joined = join_cores(core_ref, halves[i], arrived, last)
        pieces[i] = [joined, lax.ppermute(joined, "grid", to_inner)]
        last[:] = [joined]

    def send(i, part):
        expand = expand_far if part is None else expand_far[part : part + 1]
        sums[i, part] = partial_sums(expand, pieces[i], UNIT * levels, last)
        last[:] = [sums[i, part]]

    def add(i, part):
        expand = expand_near if part is None else expand_near[part : part + 1]
        far = lax.ppermute(sums[i, part], "grid", across)
        found = total_sums(expand, pieces[i], far, levels, last, LONG if i else EARLY)
        if part is None:
            totals[i, 0], totals[i, 1] = found
        else:
            totals[i, part] = found[0]
        last[:] = [found[0]]

    def share(i):
        away = lax.ppermute(totals[i, 1], "grid", to_outer)
        after = last + ([owned[i - 1]] if 0 < i < final else [])
        laid = choose(inner_ref, totals[i, 0], away, after)
        last[:] = [laid]
        owned[i] = lax.all_to_all(
            laid, ("lat", "grid"), split_axis=0, concat_axis=0, axis_index_groups=plane, tiled=True
        ).reshape((bands, 2, owned_count) + laid.shape[1:])

    final = count - 1
    rows = [UNIT * i for i in starts]
    heat(0)
    join(0)
    heat(1)
    heat(2)
    send(0, None)
    join(1)
    join(2)
    heat(3)
    send(1, None)
    join(3)
    for i in range(final):
        add(i, None)
        if i + 3 < count and i > 0:
            join(i + 3)
        if i == 0:
            send(2, None)
        if i + 4 < count:
            heat(i + 4)
        if i > 0:
            share(i - 1)
        if 0 < i and i + 2 < final:
            send(i + 2, None)
        elif i + 2 == final:
            send(final, 1)
            send(final, 0)
    add(final, 1)
    share(final - 1)
    add(final, 0)
    share(final)
    so_far = legendre_start(legendre, [owned[k] for k in range(final)], rows[:final], half_rows, last)

    position = lax.axis_index("lat") * groups + here
    taken = lax.dynamic_slice_in_dim(wave_order, position * owned_count, owned_count)
    return legendre_rest(taken, legendre, [owned[final]], rows[final:], half_rows, so_far)


def on_device(grid_state, radiation, cloud_slots, wave_order, legendre):
    levels, band_rows, lon_width = grid_state.shape
    groups = lax.axis_size("grid")
    bands = lax.axis_size("lat")
    waves = wave_order.shape[0]
    nlon = lon_width * groups
    own_rows = band_rows // groups
    chunks = 5 if own_rows % 5 == 0 else 1
    chunk_rows = own_rows // chunks

    compress, spread = factor_tables(lon_width, waves, nlon)
    rank = compress.shape[1]
    mask = cloud_mask(cloud_slots, band_rows, lon_width).reshape(groups, own_rows, lon_width)
    state = grid_state.reshape(levels, groups, own_rows, lon_width)
    basis = fourier_table(wave_order, jnp.arange(nlon, dtype=jnp.int32), nlon)
    expand = jnp.einsum(
        "rkgl,ln->krgn",
        basis.reshape(2, waves, groups, lon_width).astype(jnp.float32),
        jnp.asarray(spread),
        precision=lax.Precision.HIGHEST,
    )
    expand = (expand * (1.0 / math.sqrt(nlon))).astype(jnp.bfloat16)
    expand = expand.reshape(2 * waves, groups * rank)

    arrived = []
    for part in range(chunks):
        first = part * chunk_rows
        piece = state[:, :, first : first + chunk_rows]
        flag = mask[:, first : first + chunk_rows]
        blended = jnp.einsum("fgjl,fh->gjhl", piece, radiation, preferred_element_type=jnp.float32)
        heating = (2.0 * jnp.tanh(blended)).astype(jnp.bfloat16).astype(jnp.float32)
        heated = piece.transpose(1, 2, 0, 3).astype(jnp.float32) + heating * flag[:, :, None, :]
        packed = jnp.einsum(
            "gjhl,ln->gnjh",
            heated.astype(jnp.bfloat16),
            jnp.asarray(compress),
            preferred_element_type=jnp.float32,
        ).astype(jnp.bfloat16)
        packed = packed.reshape(groups * rank, chunk_rows * levels)
        rows = lax.all_to_all(packed, "grid", split_axis=0, concat_axis=0, tiled=True)
        coefs = jnp.dot(expand, rows, preferred_element_type=jnp.float32).astype(jnp.bfloat16)
        coefs = coefs.reshape(waves, 2, chunk_rows, levels).transpose(0, 2, 1, 3)
        coefs = coefs.reshape(waves, chunk_rows, 2 * levels)
        owned = lax.all_to_all(coefs, ("lat", "grid"), split_axis=0, concat_axis=0, tiled=True)
        arrived.append(owned.reshape(bands * groups, -1, chunk_rows, 2 * levels))

    owned_count = legendre.shape[0]
    owned = jnp.stack(arrived, axis=2).transpose(1, 0, 2, 3, 4)
    owned = owned.reshape(owned_count, bands * groups * own_rows, 2 * levels)
    position = lax.axis_index("lat") * groups + lax.axis_index("grid")
    mine = lax.dynamic_slice_in_dim(wave_order, position * owned_count, owned_count)
    spectra = jnp.einsum("kjc,kjn->kcn", owned, legendre, preferred_element_type=jnp.float32)
    degrees = jnp.arange(legendre.shape[2], dtype=jnp.int32)
    keep_mask = degrees[None, None, :] >= mine[:, None, None]
    return jnp.where(keep_mask, spectra, 0.0).astype(jnp.bfloat16)


def solution(mesh):
    in_specs = (
        P(None, "lat", "grid"),
        P(),
        P("lat", "grid", None, None),
        P(),
        P(("lat", "grid"), None, None),
    )
    out_specs = P(("lat", "grid"), None, None)

    def local(grid_state, radiation, cloud_slots, wave_order, legendre):
        half_units = sum(HALF_CHUNKS)
        fits = mesh.shape["grid"] == 8 and grid_state.shape[1] == 2 * UNIT * half_units
        program = on_line if fits else on_device
        return program(grid_state, radiation, cloud_slots, wave_order, legendre)

    return jax.shard_map(
        local, mesh=mesh, in_specs=in_specs, out_specs=out_specs, check_vma=False
    )
```
